32 devices in a mesh: groups: 2 (over y), slab: 4 (over x, core), vol: 4 (over z).
Axes of the slice: x: 2, y: 2, z: 4, core: 2. Of those that a mesh axis runs over, the one named last changes fastest.
Arguments:
- density: float32 [16, 32, 256, 256], P(('groups', 'vol'), 'slab'), parts along dimension 0, may hold values from 0.1 to 10
- weights: float32 [16], P('groups'), parts along dimension 0, may hold values from 0.5 to 2
Outputs:
- barycenter: float32 [64, 256, 256], P(('groups', 'slab')), parts along dimension 0
- scaling: float32 [16, 32, 256, 256], P(('groups', 'vol'), 'slab'), parts along dimension 0
The draws below stay inside these ranges and needn't reach their ends.
There are 2 independent parts, one for each index of `groups`. The reference program is written for one: setup_inputs(seed, part) draws one part's arguments, and reference() takes and returns one part's arrays. A program takes and returns all parts, laid end to end along the dimension named above; each array names one. Nothing has to cross between parts.
All inputs are finite; a program needn't handle non-finite values.
Results may differ from the reference program's by a relative error of at most 0.00002.
Values sent between devices are 32-bit elements; how exact they have to be, the bound alone decides.
A program may use at most 64 MiB of HBM per device.

```python
import math
import jax
import jax.numpy as jnp
import numpy as np
from jax import lax

NX = 256
NY = 256
ITERS = 2
VOLS = 8
NZ = 32


def block_scale(stream_key, extent, shards, low, high):
    factor_of, own = 1.0, jax.random.fold_in(stream_key, 6)
    for position, parts in shards:
        heights = jnp.exp(jax.random.uniform(jax.random.fold_in(own, position), (parts,), jnp.float32, low / len(shards), high / len(shards)))
        factor_of = factor_of * jnp.repeat(heights, extent[position] // parts).reshape([-1 if axis == position else 1 for axis in range(len(extent))])
    return factor_of


def setup_inputs(seed: int = 0, part: int = 0) -> dict:
    key_of = jax.random.split(jax.random.key(seed), 3)
    own_keys = jax.random.split(jax.random.fold_in(key_of[2], part), 3)
    density = jnp.clip(jnp.exp(math.log(10.0) - 4.6051702 * jax.random.uniform(own_keys[0], (VOLS, NZ, NX, NY), jnp.float32) ** block_scale(own_keys[0], (VOLS, NZ, NX, NY), ((0, 4), (1, 4)), -0.2, 0.2)), 0.1, 10.0)
    weights = jnp.clip(jnp.exp(jax.random.uniform(own_keys[1], (VOLS,), jnp.float32, math.log(0.5), math.log(2.0))), 0.5, 2.0)
    return {"density": density, "weights": weights}


gauss_raw = np.exp(-0.5 * np.arange(-2, 3) ** 2)
kernel_taps = [float(entry) for entry in gauss_raw / gauss_raw.sum()]


def blur_valid(volume, along):
    length = volume.shape[along] - 4
    total = kernel_taps[0] * lax.slice_in_dim(volume, 0, length, axis=along)
    for offset in range(1, 5):
        total = total + kernel_taps[offset] * lax.slice_in_dim(volume, offset, offset + length, axis=along)
    return total


def blur_zero(volume, along):
    widths = [(0, 0)] * volume.ndim
    widths[along] = (2, 2)
    return blur_valid(jnp.pad(volume, widths), along)


def heat(volume):
    return blur_zero(blur_zero(blur_zero(volume, 0), 1), 2)


def reference(density, weights):
    norm_weights = weights / jnp.sum(weights)
    scaling = jnp.ones_like(density)
    center = jnp.zeros(density.shape[1:], jnp.float32)
    for sweep in range(ITERS):
        def per_volume(total, items):
            dens, scal, weight = items
            quotient = dens / heat(scal)
            marginal = scal * heat(quotient)
            return total + weight * jnp.log(marginal), marginal

        start = jnp.zeros(density.shape[1:], jnp.float32)
        log_mean, marginal = lax.scan(per_volume, start, (density, scaling, norm_weights))
        center = jnp.exp(log_mean)
        scaling = scaling * center[None] / marginal
    return center, scaling
```

```python
import functools

import jax
import jax.numpy as jnp
import numpy as np
from jax import lax
from jax.experimental import pallas as pl
from jax.experimental.pallas import tpu as pltpu
from jax.sharding import PartitionSpec as P

ITERS = 2
HALO = 2
CHUNKS = 4

gauss_raw = np.exp(-0.5 * np.arange(-2, 3) ** 2)
kernel_taps = [float(entry) for entry in gauss_raw / gauss_raw.sum()]
edge_sums = [sum(kernel_taps[2:]), sum(kernel_taps[1:]), sum(kernel_taps)]


def per_distance(distance):
    inverse = [1.0 / entry for entry in edge_sums]
    inner = jnp.where(distance == 1, inverse[1], inverse[2])
    return jnp.where(distance == 0, inverse[0], inner).astype(jnp.float32)


def band(size):
    rows = lax.broadcasted_iota(jnp.int32, (size, size), 0)
    gap = jnp.abs(rows - lax.broadcasted_iota(jnp.int32, (size, size), 1))
    inner = jnp.where(gap == 1, kernel_taps[1], jnp.where(gap == 2, kernel_taps[0], 0.0))
    return jnp.where(gap == 0, kernel_taps[2], inner).astype(jnp.float32)


def kernel(
    slabs, vols,
    weights, density, center_out, scaling_out,
    dens, scal, quot, marg, cent, acc, outer, inner, inverse, band_x, band_y,
    local_sem, out_sem, d_send, d_recv, s_send, s_recv, q_send, q_recv,
    up_send, down_send, outer_recv, inner_recv,
):
    own, nz, nx, ny = density.shape
    total_nz = nz * slabs
    rows = nx // CHUNKS
    steps = nz * CHUNKS
    slab, vol = lax.axis_index("slab"), lax.axis_index("vol")
    half = vols // 2
    low_side = vol < half
    inward = jnp.where(low_side, vol + 1, vol - 1)
    outward = jnp.where(low_side, vol - 1, vol + 1)
    depth = jnp.where(low_side, half - 1 - vol, vol - half)
    is_center = depth == 0
    has_outer = depth < half - 1
    lag = 2 + 5 * depth
    has_low, has_high = slab > 0, slab < slabs - 1

    barrier = pltpu.get_barrier_semaphore()

    def greet(device):
        pl.semaphore_signal(barrier, inc=1, device_id=device, device_id_type=pl.DeviceIdType.MESH)

    pl.when(has_low)(lambda: greet({"slab": slab - 1}))
    pl.when(has_high)(lambda: greet({"slab": slab + 1}))
    greet({"vol": inward})
    pl.when(has_outer)(lambda: greet({"vol": outward}))

    loads = [
        pltpu.make_async_copy(density.at[k], dens.at[k, pl.ds(HALO, nz)], local_sem.at[k])
        for k in range(own)
    ]
    for load in loads:
        load.start()

    def remote(src, dst, send, recv, device):
        return pltpu.make_async_remote_copy(
            src_ref=src, dst_ref=dst, send_sem=send, recv_sem=recv,
            device_id=device, device_id_type=pl.DeviceIdType.MESH,
        )

    def density_low(k):
        return remote(
            density.at[k, pl.ds(0, HALO)], dens.at[k, pl.ds(nz + HALO, HALO)],
            d_send.at[0, k], d_recv.at[0, k], {"slab": slab - 1},
        )

    def density_high(k):
        return remote(
            density.at[k, pl.ds(nz - HALO, HALO)], dens.at[k, pl.ds(0, HALO)],
            d_send.at[1, k], d_recv.at[1, k], {"slab": slab + 1},
        )

    def plane_low(buf, send, recv, k, p):
        return remote(
            buf.at[k, p + HALO], buf.at[k, p + HALO + nz],
            send.at[0, k, p], recv.at[0, k, p], {"slab": slab - 1},
        )

    def plane_high(buf, send, recv, k, p):
        at = p - (nz - HALO)
        return remote(
            buf.at[k, p + HALO], buf.at[k, at],
            send.at[1, k, at], recv.at[1, k, at], {"slab": slab + 1},
        )

    waits = jnp.where(has_low, 1, 0) + jnp.where(has_high, 1, 0) + jnp.where(has_outer, 2, 1)
    pl.semaphore_wait(barrier, waits)

    @pl.when(has_low)
    def _():
        for k in range(own):
            density_low(k).start()

    @pl.when(has_high)
    def _():
        for k in range(own):
            density_high(k).start()

    @pl.when(jnp.logical_not(has_low))
    def _():
        for buf in (dens, scal, quot):
            buf[:, 0:HALO] = jnp.zeros((own, HALO, nx, ny), jnp.float32)

    @pl.when(jnp.logical_not(has_high))
    def _():
        for buf in (dens, scal, quot):
            buf[:, nz + HALO :] = jnp.zeros((own, HALO, nx, ny), jnp.float32)

    band_x[...] = band(nx)
    band_y[...] = band(ny)
    at_x = lax.broadcasted_iota(jnp.int32, (nx, ny), 0)
    at_y = lax.broadcasted_iota(jnp.int32, (nx, ny), 1)
    inverse[...] = per_distance(jnp.minimum(at_x, nx - 1 - at_x)) * per_distance(
        jnp.minimum(at_y, ny - 1 - at_y)
    )

    count = weights.shape[0]
    weight_sum = weights[0]
    for k in range(1, count):
        weight_sum = weight_sum + weights[k]
    norm = [
        jnp.full((1, ny), weights[vol * own + k], jnp.float32)
        / jnp.full((1, ny), weight_sum, jnp.float32)
        for k in range(own)
    ]

    def in_plane(value):
        dot = functools.partial(
            jnp.dot, precision=lax.Precision.HIGHEST, preferred_element_type=jnp.float32
        )
        return dot(band_x[...], dot(value, band_y[...]))

    def along_z(buf, k, p):
        total = kernel_taps[0] * (buf[k, p] + buf[k, p + 4])
        total = total + kernel_taps[1] * (buf[k, p + 1] + buf[k, p + 3])
        return total + kernel_taps[2] * buf[k, p + 2]

    def faces(i):
        return i // 2 + (i % 2) * (nz - 1 - 2 * (i // 2))

    def order_first(i):
        late, last = (i + nz - 2) // nz, (i + nz - 6) // nz
        return (1 - late) * (i + 2) + (late - last) * faces(jnp.maximum(i - 2, 0)) + last * (i - 2)

    def order_faces(i):
        late = (i + nz - 4) // nz
        return (1 - late) * faces(i) + late * (i - 2)

    def order_second(i):
        late = (i + 4) // nz
        return (1 - late) * (i + 2) + late * faces(jnp.maximum(i - (nz - 4), 0))

    def up_center(t, g):
        return remote(
            acc.at[t, g], inner.at[t, g], up_send.at[t, g], inner_recv.at[t, g], {"vol": inward}
        )

    def up_other(t, g):
        return remote(
            acc.at[t, g], outer.at[t, g], up_send.at[t, g], outer_recv.at[t, g], {"vol": inward}
        )

    def down_copy(t, g):
        return remote(
            inner.at[t, g], inner.at[t, g], down_send.at[t, g], inner_recv.at[t, g],
            {"vol": outward},
        )

    def up(t, g):
        @pl.when(has_outer)
        def _():
            up_other(t, g).wait_recv()
            acc[t, g] = acc[t, g] + outer[t, g]

        pl.when(is_center)(lambda: up_center(t, g).start())
        pl.when(jnp.logical_not(is_center))(lambda: up_other(t, g).start())

    def down(t, g, use):
        down_copy(t, g).wait_recv()

        @pl.when(is_center)
        def _():
            inner[t, g] = inner[t, g] + acc[t, g]

        pl.when(has_outer)(lambda: down_copy(t, g).start())
        use(g)

    def all_reduce(t, order, compute, use):
        def step(i, _):
            part = compute(i, order(i))
            for c in range(CHUNKS):
                acc[t, i * CHUNKS + c] = part[c * rows : (c + 1) * rows]

            def chunk(c, _):
                g = i * CHUNKS + c
                up(t, g)
                pl.when(g >= lag)(lambda: down(t, g - lag, use))
                return 0

            lax.fori_loop(0, CHUNKS, chunk, 0)
            return 0

        lax.fori_loop(0, nz, step, 0)

        def tail(g, _):
            down(t, g, use)
            return 0

        lax.fori_loop(steps - lag, steps, tail, 0)

    def weighted(k, value):
        return norm[k] * jnp.log(value)

    for load in loads:
        load.wait()

    def first_compute(i, p):
        @pl.when(i == 2)
        def _():
            @pl.when(has_low)
            def _():
                for k in range(own):
                    density_high(k).wait_recv()

            @pl.when(has_high)
            def _():
                for k in range(own):
                    density_low(k).wait_recv()

        scale = []
        for offset in range(5):
            z = slab * nz + p + offset - HALO
            scale.append(kernel_taps[offset] * per_distance(jnp.minimum(z, total_nz - 1 - z)))
        part = None
        for k in range(own):
            value = scale[0] * dens[k, p]
            for offset in range(1, 5):
                value = value + scale[offset] * dens[k, p + offset]
            spread = in_plane(value * inverse[...])
            marg[k, p] = spread
            term = weighted(k, spread)
            part = term if part is None else part + term
        return part

    def send_face(buf, send, recv, p):
        @pl.when(jnp.logical_and(has_low, p < HALO))
        def _():
            for k in range(own):
                plane_low(buf, send, recv, k, p).start()

        @pl.when(jnp.logical_and(has_high, p >= nz - HALO))
        def _():
            for k in range(own):
                plane_high(buf, send, recv, k, p).start()

    def wait_faces(buf, send, recv):
        @pl.when(has_low)
        def _():
            for k in range(own):
                for p in range(nz - HALO, nz):
                    plane_high(buf, send, recv, k, p).wait_recv()

        @pl.when(has_high)
        def _():
            for k in range(own):
                for p in range(HALO):
                    plane_low(buf, send, recv, k, p).wait_recv()

    def wait_sent(buf, send, recv):
        @pl.when(has_low)
        def _():
            for k in range(own):
                for p in range(HALO):
                    plane_low(buf, send, recv, k, p).wait_send()

        @pl.when(has_high)
        def _():
            for k in range(own):
                for p in range(nz - HALO, nz):
                    plane_high(buf, send, recv, k, p).wait_send()

    def first_use(g):
        p, c = order_first(g // CHUNKS), g % CHUNKS
        at = pl.ds(pl.multiple_of(c * rows, rows), rows)
        center = jnp.exp(inner[0, g])
        for k in range(own):
            scal[k, p + HALO, at] = center / marg[k, p, at]
        pl.when(c == CHUNKS - 1)(lambda: send_face(scal, s_send, s_recv, p))

    all_reduce(0, order_first, first_compute, first_use)

    wait_faces(scal, s_send, s_recv)

    def quotient(i, _):
        p = order_faces(i)
        for k in range(own):
            quot[k, p + HALO] = dens[k, p + HALO] / in_plane(along_z(scal, k, p))
        send_face(quot, q_send, q_recv, p)
        return 0

    lax.fori_loop(0, nz, quotient, 0)

    def second_compute(i, p):
        pl.when(i == nz - 4)(lambda: wait_faces(quot, q_send, q_recv))
        part = None
        for k in range(own):
            marginal = scal[k, p + HALO] * in_plane(along_z(quot, k, p))
            marg[k, p] = marginal
            term = weighted(k, marginal)
            part = term if part is None else part + term
        return part

    def center_store(p):
        return pltpu.make_async_copy(cent.at[p], center_out.at[p], out_sem.at[own, p])

    def scaling_store(k, p):
        return pltpu.make_async_copy(marg.at[k, p], scaling_out.at[k, p], out_sem.at[k, p])

    def second_use(g):
        p, c = order_second(g // CHUNKS), g % CHUNKS
        at = pl.ds(pl.multiple_of(c * rows, rows), rows)
        center = jnp.exp(inner[1, g])
        cent[p, at] = center
        for k in range(own):
            marg[k, p, at] = scal[k, p + HALO, at] * center / marg[k, p, at]

        @pl.when(c == CHUNKS - 1)
        def _():
            center_store(p).start()
            for k in range(own):
                scaling_store(k, p).start()

    all_reduce(1, order_second, second_compute, second_use)

    @pl.when(has_low)
    def _():
        for k in range(own):
            density_low(k).wait_send()

    @pl.when(has_high)
    def _():
        for k in range(own):
            density_high(k).wait_send()

    wait_sent(scal, s_send, s_recv)
    wait_sent(quot, q_send, q_recv)

    def drain(g, _):
        for t in range(ITERS):
            up_other(t, g).wait_send()
            pl.when(has_outer)(lambda: down_copy(t, g).wait_send())
        return 0

    lax.fori_loop(0, steps, drain, 0)

    def stored(p, _):
        center_store(p).wait()
        for k in range(own):
            scaling_store(k, p).wait()
        return 0

    lax.fori_loop(0, nz, stored, 0)


def per_device(slabs, vols, density, weights):
    own, nz, nx, ny = density.shape
    steps, rows = nz * CHUNKS, nx // CHUNKS
    padded = pltpu.VMEM((own, nz + 2 * HALO, nx, ny), jnp.float32)
    chunks = pltpu.VMEM((ITERS, steps, rows, ny), jnp.float32)
    dma = pltpu.SemaphoreType.DMA
    return pl.pallas_call(
        functools.partial(kernel, slabs, vols),
        out_shape=(
            jax.ShapeDtypeStruct((nz, nx, ny), jnp.float32),
            jax.ShapeDtypeStruct(density.shape, jnp.float32),
        ),
        in_specs=[pl.BlockSpec(memory_space=pltpu.SMEM), pl.BlockSpec(memory_space=pl.ANY)],
        out_specs=(pl.BlockSpec(memory_space=pl.ANY), pl.BlockSpec(memory_space=pl.ANY)),
        scratch_shapes=[
            padded, padded, padded,
            pltpu.VMEM((own, nz, nx, ny), jnp.float32),
            pltpu.VMEM((nz, nx, ny), jnp.float32),
            chunks, chunks, chunks,
            pltpu.VMEM((nx, ny), jnp.float32),
            pltpu.VMEM((nx, nx), jnp.float32),
            pltpu.VMEM((ny, ny), jnp.float32),
            dma((own,)), dma((own + 1, nz)),
            dma((2, own)), dma((2, own)),
            dma((2, own, HALO)), dma((2, own, HALO)),
            dma((2, own, HALO)), dma((2, own, HALO)),
            dma((ITERS, steps)), dma((ITERS, steps)),
            dma((ITERS, steps)), dma((ITERS, steps)),
        ],
        compiler_params=pltpu.CompilerParams(
            collective_id=0, has_side_effects=True, vmem_limit_bytes=52 * 1024 * 1024
        ),
    )(weights, density)


def solution(mesh):
    in_specs = (P(("groups", "vol"), "slab", None, None), P("groups"))
    out_specs = (P(("groups", "slab"), None, None), P(("groups", "vol"), "slab", None, None))
    body = functools.partial(per_device, mesh.shape["slab"], mesh.shape["vol"])
    return jax.shard_map(
        body, mesh=mesh, in_specs=in_specs, out_specs=out_specs, check_vma=False
    )
```

```python
import functools

import jax
import jax.numpy as jnp
import numpy as np
from jax import lax
from jax.experimental import pallas as pl
from jax.experimental.pallas import tpu as pltpu
from jax.sharding import PartitionSpec as P

ITERS = 2
HALO = 2
CHUNKS = 4

gauss_raw = np.exp(-0.5 * np.arange(-2, 3) ** 2)
kernel_taps = [float(entry) for entry in gauss_raw / gauss_raw.sum()]
edge_sums = [sum(kernel_taps[2:]), sum(kernel_taps[1:]), sum(kernel_taps)]


def per_distance(distance):
    inverse = [1.0 / entry for entry in edge_sums]
    inner = jnp.where(distance == 1, inverse[1], inverse[2])
    return jnp.where(distance == 0, inverse[0], inner).astype(jnp.float32)


def band(size):
    rows = lax.broadcasted_iota(jnp.int32, (size, size), 0)
    gap = jnp.abs(rows - lax.broadcasted_iota(jnp.int32, (size, size), 1))
    inner = jnp.where(gap == 1, kernel_taps[1], jnp.where(gap == 2, kernel_taps[0], 0.0))
    return jnp.where(gap == 0, kernel_taps[2], inner).astype(jnp.float32)


def kernel(
    slabs, vols,
    weights, density, center_out, scaling_out,
    dens, scal, quot, marg, cent, acc, outer, inner, inverse, band_x, band_y,
    local_sem, out_sem, d_send, d_recv, s_send, s_recv, q_send, q_recv,
    up_send, down_send, outer_recv, inner_recv,
):
    own, nz, nx, ny = density.shape
    total_nz = nz * slabs
    rows = nx // CHUNKS
    steps = nz * CHUNKS
    slab, vol = lax.axis_index("slab"), lax.axis_index("vol")
    half = vols // 2
    low_side = vol < half
    inward = jnp.where(low_side, vol + 1, vol - 1)
    outward = jnp.where(low_side, vol - 1, vol + 1)
    depth = jnp.where(low_side, half - 1 - vol, vol - half)
    is_center = depth == 0
    early = depth > 0
    has_outer = depth < half - 1
    lag = jnp.minimum(4 + 10 * depth, steps)
    has_low, has_high = slab > 0, slab < slabs - 1

    barrier = pltpu.get_barrier_semaphore()

    def greet(device):
        pl.semaphore_signal(barrier, inc=1, device_id=device, device_id_type=pl.DeviceIdType.MESH)

    pl.when(has_low)(lambda: greet({"slab": slab - 1}))
    pl.when(has_high)(lambda: greet({"slab": slab + 1}))
    greet({"vol": inward})
    pl.when(has_outer)(lambda: greet({"vol": outward}))

    loads = [
        pltpu.make_async_copy(density.at[k], dens.at[k, pl.ds(HALO, nz)], local_sem.at[k])
        for k in range(own)
    ]
    for load in loads:
        load.start()

    def remote(src, dst, send, recv, device):
        return pltpu.make_async_remote_copy(
            src_ref=src, dst_ref=dst, send_sem=send, recv_sem=recv,
            device_id=device, device_id_type=pl.DeviceIdType.MESH,
        )

    def density_low(k):
        return remote(
            density.at[k, pl.ds(0, HALO)], dens.at[k, pl.ds(nz + HALO, HALO)],
            d_send.at[0, k], d_recv.at[0, k], {"slab": slab - 1},
        )

    def density_high(k):
        return remote(
            density.at[k, pl.ds(nz - HALO, HALO)], dens.at[k, pl.ds(0, HALO)],
            d_send.at[1, k], d_recv.at[1, k], {"slab": slab + 1},
        )

    def plane_low(buf, send, recv, k, p):
        return remote(
            buf.at[k, p + HALO], buf.at[k, p + HALO + nz],
            send.at[0, k, p], recv.at[0, k, p], {"slab": slab - 1},
        )

    def plane_high(buf, send, recv, k, p):
        at = p - (nz - HALO)
        return remote(
            buf.at[k, p + HALO], buf.at[k, at],
            send.at[1, k, at], recv.at[1, k, at], {"slab": slab + 1},
        )

    waits = jnp.where(has_low, 1, 0) + jnp.where(has_high, 1, 0) + jnp.where(has_outer, 2, 1)
    pl.semaphore_wait(barrier, waits)

    @pl.when(has_low)
    def _():
        for k in range(own):
            density_low(k).start()

    @pl.when(has_high)
    def _():
        for k in range(own):
            density_high(k).start()

    @pl.when(jnp.logical_not(has_low))
    def _():
        for buf in (dens, scal, quot):
            buf[:, 0:HALO] = jnp.zeros((own, HALO, nx, ny), jnp.float32)

    @pl.when(jnp.logical_not(has_high))
    def _():
        for buf in (dens, scal, quot):
            buf[:, nz + HALO :] = jnp.zeros((own, HALO, nx, ny), jnp.float32)

    for taps, size in ((band_x, nx), (band_y, ny)):
        whole = band(size)
        high = whole.astype(jnp.bfloat16)
        taps[0] = high
        taps[1] = (whole - high.astype(jnp.float32)).astype(jnp.bfloat16)
    at_x = lax.broadcasted_iota(jnp.int32, (nx, ny), 0)
    at_y = lax.broadcasted_iota(jnp.int32, (nx, ny), 1)
    inverse[...] = per_distance(jnp.minimum(at_x, nx - 1 - at_x)) * per_distance(
        jnp.minimum(at_y, ny - 1 - at_y)
    )

    count = weights.shape[0]
    weight_sum = weights[0]
    for k in range(1, count):
        weight_sum = weight_sum + weights[k]
    norm = [
        jnp.full((1, ny), weights[vol * own + k], jnp.float32)
        / jnp.full((1, ny), weight_sum, jnp.float32)
        for k in range(own)
    ]

    def split(value):
        high = value.astype(jnp.bfloat16)
        return high, (value - high.astype(jnp.float32)).astype(jnp.bfloat16)

    def dot(a, b):
        return jnp.dot(a, b, preferred_element_type=jnp.float32)

    def in_plane(value):
        high, low = split(value)
        blurred = dot(high, band_y[0]) + (dot(high, band_y[1]) + dot(low, band_y[0]))
        high, low = split(blurred)
        return dot(band_x[0], high) + (dot(band_x[1], high) + dot(band_x[0], low))

    def along_z(buf, k, p):
        total = kernel_taps[0] * (buf[k, p] + buf[k, p + 4])
        total = total + kernel_taps[1] * (buf[k, p + 1] + buf[k, p + 3])
        return total + kernel_taps[2] * buf[k, p + 2]

    def faces(i):
        return i // 2 + (i % 2) * (nz - 1 - 2 * (i // 2))

    def order_first(i):
        late, last = (i + nz - 2) // nz, (i + nz - 6) // nz
        return (1 - late) * (i + 2) + (late - last) * faces(jnp.maximum(i - 2, 0)) + last * (i - 2)

    def order_second(i):
        late = (i + 4) // nz
        return (1 - late) * (i + 2) + late * faces(jnp.maximum(i - (nz - 4), 0))

    def up_center(t, g):
        return remote(
            acc.at[t, g], inner.at[t, g], up_send.at[t, g], inner_recv.at[t, g], {"vol": inward}
        )

    def up_other(t, g):
        return remote(
            acc.at[t, g], outer.at[t, g], up_send.at[t, g], outer_recv.at[t, g], {"vol": inward}
        )

    def down_copy(t, g):
        return remote(
            inner.at[t, g], inner.at[t, g], down_send.at[t, g], inner_recv.at[t, g],
            {"vol": outward},
        )

    def up(t, g):
        @pl.when(has_outer)
        def _():
            up_other(t, g).wait_recv()
            acc[t, g] = acc[t, g] + outer[t, g]

        pl.when(is_center)(lambda: up_center(t, g).start())
        pl.when(jnp.logical_not(is_center))(lambda: up_other(t, g).start())

    def down(t, g, use):
        down_copy(t, g).wait_recv()

        @pl.when(is_center)
        def _():
            inner[t, g] = inner[t, g] + acc[t, g]

        pl.when(has_outer)(lambda: down_copy(t, g).start())
        use(g)

    def all_reduce(t, order, compute, use):
        def step(i, _):
            part = compute(i, order(i))
            for c in range(CHUNKS):
                acc[t, i * CHUNKS + c] = part[c * rows : (c + 1) * rows]

            def chunk(c, _):
                g = i * CHUNKS + c
                up(t, g)
                pl.when(g >= lag)(lambda: down(t, g - lag, use))
                return 0

            lax.fori_loop(0, CHUNKS, chunk, 0)
            return 0

        lax.fori_loop(0, nz, step, 0)

        def tail(g, _):
            down(t, g, use)
            return 0

        lax.fori_loop(steps - lag, steps, tail, 0)

    def weighted(k, value):
        return norm[k] * jnp.log(value)

    for load in loads:
        load.wait()

    def first_compute(i, p):
        @pl.when(i == 2)
        def _():
            @pl.when(has_low)
            def _():
                for k in range(own):
                    density_high(k).wait_recv()

            @pl.when(has_high)
            def _():
                for k in range(own):
                    density_low(k).wait_recv()

        scale = []
        for offset in range(5):
            z = slab * nz + p + offset - HALO
            scale.append(kernel_taps[offset] * per_distance(jnp.minimum(z, total_nz - 1 - z)))
        part = None
        for k in range(own):
            value = scale[0] * dens[k, p]
            for offset in range(1, 5):
                value = value + scale[offset] * dens[k, p + offset]
            spread = in_plane(value * inverse[...])
            marg[k, p] = spread
            term = weighted(k, spread)
            part = term if part is None else part + term
        return part

    def send_face(buf, send, recv, p):
        @pl.when(jnp.logical_and(has_low, p < HALO))
        def _():
            for k in range(own):
                plane_low(buf, send, recv, k, p).start()

        @pl.when(jnp.logical_and(has_high, p >= nz - HALO))
        def _():
            for k in range(own):
                plane_high(buf, send, recv, k, p).start()

    def wait_low(buf, send, recv):
        @pl.when(has_low)
        def _():
            for k in range(own):
                for p in range(nz - HALO, nz):
                    plane_high(buf, send, recv, k, p).wait_recv()

    def wait_high(buf, send, recv):
        @pl.when(has_high)
        def _():
            for k in range(own):
                for p in range(HALO):
                    plane_low(buf, send, recv, k, p).wait_recv()

    def wait_sent(buf, send, recv):
        @pl.when(has_low)
        def _():
            for k in range(own):
                for p in range(HALO):
                    plane_low(buf, send, recv, k, p).wait_send()

        @pl.when(has_high)
        def _():
            for k in range(own):
                for p in range(nz - HALO, nz):
                    plane_high(buf, send, recv, k, p).wait_send()

    def quotient(p):
        for k in range(own):
            quot[k, p + HALO] = dens[k, p + HALO] / in_plane(along_z(scal, k, p))
        send_face(quot, q_send, q_recv, p)

    def quotients(start, stop):
        def one(p, _):
            quotient(p)
            return 0

        lax.fori_loop(start, stop, one, 0)

    def quotients_low():
        wait_low(scal, s_send, s_recv)
        quotients(0, HALO)

    def first_use(g):
        i, c = g // CHUNKS, g % CHUNKS
        p = order_first(i)
        at = pl.ds(pl.multiple_of(c * rows, rows), rows)
        center = jnp.exp(inner[0, g])
        for k in range(own):
            scal[k, p + HALO, at] = center / marg[k, p, at]

        @pl.when(c == CHUNKS - 1)
        def _():
            send_face(scal, s_send, s_recv, p)
            pl.when(jnp.logical_and(i == nz - 2, early))(quotients_low)

    all_reduce(0, order_first, first_compute, first_use)

    pl.when(jnp.logical_not(early))(quotients_low)
    quotients(HALO, HALO + 3)
    wait_high(scal, s_send, s_recv)
    quotients(nz - 1, nz)

    def second_compute(i, p):
        @pl.when(jnp.logical_and(i >= 1, i < nz - 5))
        def _():
            quotient(i + 4)

        @pl.when(i == nz - 4)
        def _():
            wait_low(quot, q_send, q_recv)
            wait_high(quot, q_send, q_recv)

        part = None
        for k in range(own):
            marginal = scal[k, p + HALO] * in_plane(along_z(quot, k, p))
            marg[k, p] = marginal
            term = weighted(k, marginal)
            part = term if part is None else part + term
        return part

    def center_store(p):
        return pltpu.make_async_copy(cent.at[p], center_out.at[p], out_sem.at[own, p])

    def scaling_store(k, p):
        return pltpu.make_async_copy(marg.at[k, p], scaling_out.at[k, p], out_sem.at[k, p])

    def second_use(g):
        p, c = order_second(g // CHUNKS), g % CHUNKS
        at = pl.ds(pl.multiple_of(c * rows, rows), rows)
        center = jnp.exp(inner[1, g])
        cent[p, at] = center
        for k in range(own):
            marg[k, p, at] = scal[k, p + HALO, at] * center / marg[k, p, at]

        @pl.when(c == CHUNKS - 1)
        def _():
            center_store(p).start()
            for k in range(own):
                scaling_store(k, p).start()

    all_reduce(1, order_second, second_compute, second_use)

    @pl.when(has_low)
    def _():
        for k in range(own):
            density_low(k).wait_send()

    @pl.when(has_high)
    def _():
        for k in range(own):
            density_high(k).wait_send()

    wait_sent(scal, s_send, s_recv)
    wait_sent(quot, q_send, q_recv)

    def drain(g, _):
        for t in range(ITERS):
            up_other(t, g).wait_send()
            pl.when(has_outer)(lambda: down_copy(t, g).wait_send())
        return 0

    lax.fori_loop(0, steps, drain, 0)

    def stored(p, _):
        center_store(p).wait()
        for k in range(own):
            scaling_store(k, p).wait()
        return 0

    lax.fori_loop(0, nz, stored, 0)


def per_device(slabs, vols, density, weights):
    own, nz, nx, ny = density.shape
    steps, rows = nz * CHUNKS, nx // CHUNKS
    padded = pltpu.VMEM((own, nz + 2 * HALO, nx, ny), jnp.float32)
    chunks = pltpu.VMEM((ITERS, steps, rows, ny), jnp.float32)
    dma = pltpu.SemaphoreType.DMA
    return pl.pallas_call(
        functools.partial(kernel, slabs, vols),
        out_shape=(
            jax.ShapeDtypeStruct((nz, nx, ny), jnp.float32),
            jax.ShapeDtypeStruct(density.shape, jnp.float32),
        ),
        in_specs=[pl.BlockSpec(memory_space=pltpu.SMEM), pl.BlockSpec(memory_space=pl.ANY)],
        out_specs=(pl.BlockSpec(memory_space=pl.ANY), pl.BlockSpec(memory_space=pl.ANY)),
        scratch_shapes=[
            padded, padded, padded,
            pltpu.VMEM((own, nz, nx, ny), jnp.float32),
            pltpu.VMEM((nz, nx, ny), jnp.float32),
            chunks, chunks, chunks,
            pltpu.VMEM((nx, ny), jnp.float32),
            pltpu.VMEM((2, nx, nx), jnp.bfloat16),
            pltpu.VMEM((2, ny, ny), jnp.bfloat16),
            dma((own,)), dma((own + 1, nz)),
            dma((2, own)), dma((2, own)),
            dma((2, own, HALO)), dma((2, own, HALO)),
            dma((2, own, HALO)), dma((2, own, HALO)),
            dma((ITERS, steps)), dma((ITERS, steps)),
            dma((ITERS, steps)), dma((ITERS, steps)),
        ],
        compiler_params=pltpu.CompilerParams(
            collective_id=0, has_side_effects=True, vmem_limit_bytes=52 * 1024 * 1024
        ),
    )(weights, density)


def solution(mesh):
    in_specs = (P(("groups", "vol"), "slab", None, None), P("groups"))
    out_specs = (P(("groups", "slab"), None, None), P(("groups", "vol"), "slab", None, None))
    body = functools.partial(per_device, mesh.shape["slab"], mesh.shape["vol"])
    return jax.shard_map(
        body, mesh=mesh, in_specs=in_specs, out_specs=out_specs, check_vma=False
    )
```

```python
import functools

import jax
import jax.numpy as jnp
import numpy as np
from jax import lax
from jax.experimental import pallas as pl
from jax.experimental.pallas import tpu as pltpu
from jax.sharding import PartitionSpec as P

ITERS = 2
HALO = 2
CHUNKS = 4

gauss_raw = np.exp(-0.5 * np.arange(-2, 3) ** 2)
kernel_taps = [float(entry) for entry in gauss_raw / gauss_raw.sum()]
edge_sums = [sum(kernel_taps[2:]), sum(kernel_taps[1:]), sum(kernel_taps)]


def per_distance(distance):
    inverse = [1.0 / entry for entry in edge_sums]
    inner = jnp.where(distance == 1, inverse[1], inverse[2])
    return jnp.where(distance == 0, inverse[0], inner).astype(jnp.float32)


def band(size):
    rows = lax.broadcasted_iota(jnp.int32, (size, size), 0)
    gap = jnp.abs(rows - lax.broadcasted_iota(jnp.int32, (size, size), 1))
    inner = jnp.where(gap == 1, kernel_taps[1], jnp.where(gap == 2, kernel_taps[0], 0.0))
    return jnp.where(gap == 0, kernel_taps[2], inner).astype(jnp.float32)


def kernel(
    slabs, vols,
    weights, density, center_out, scaling_out,
    dens, scal, quot, marg, cent, acc, outer, inner, inverse, band_x, band_y,
    local_sem, out_sem, d_send, d_recv, s_send, s_recv, q_send, q_recv,
    up_send, down_send, outer_recv, inner_recv,
):
    own, nz, nx, ny = density.shape
    total_nz = nz * slabs
    rows = nx // CHUNKS
    steps = nz * CHUNKS
    slab, vol = lax.axis_index("slab"), lax.axis_index("vol")
    half = vols // 2
    low_side = vol < half
    inward = jnp.where(low_side, vol + 1, vol - 1)
    outward = jnp.where(low_side, vol - 1, vol + 1)
    depth = jnp.where(low_side, half - 1 - vol, vol - half)
    is_center = depth == 0
    early = depth > 0
    has_outer = depth < half - 1
    lag = jnp.minimum(4 + 10 * depth, steps)
    has_low, has_high = slab > 0, slab < slabs - 1

    barrier = pltpu.get_barrier_semaphore()

    def greet(device):
        pl.semaphore_signal(barrier, inc=1, device_id=device, device_id_type=pl.DeviceIdType.MESH)

    pl.when(has_low)(lambda: greet({"slab": slab - 1}))
    pl.when(has_high)(lambda: greet({"slab": slab + 1}))
    greet({"vol": inward})
    pl.when(has_outer)(lambda: greet({"vol": outward}))

    loads = [
        pltpu.make_async_copy(density.at[k], dens.at[k, pl.ds(HALO, nz)], local_sem.at[k])
        for k in range(own)
    ]
    for load in loads:
        load.start()

    def remote(src, dst, send, recv, device):
        return pltpu.make_async_remote_copy(
            src_ref=src, dst_ref=dst, send_sem=send, recv_sem=recv,
            device_id=device, device_id_type=pl.DeviceIdType.MESH,
        )

    def density_low(k, near):
        return remote(
            density.at[k, near], dens.at[k, nz + HALO + near],
            d_send.at[0, k, near], d_recv.at[0, k, near], {"slab": slab - 1},
        )

    def density_high(k, near):
        return remote(
            density.at[k, nz - 1 - near], dens.at[k, HALO - 1 - near],
            d_send.at[1, k, near], d_recv.at[1, k, near], {"slab": slab + 1},
        )

    def plane_low(buf, send, recv, k, p):
        return remote(
            buf.at[k, p + HALO], buf.at[k, p + HALO + nz],
            send.at[0, k, p], recv.at[0, k, p], {"slab": slab - 1},
        )

    def plane_high(buf, send, recv, k, p):
        at = p - (nz - HALO)
        return remote(
            buf.at[k, p + HALO], buf.at[k, at],
            send.at[1, k, at], recv.at[1, k, at], {"slab": slab + 1},
        )

    waits = jnp.where(has_low, 1, 0) + jnp.where(has_high, 1, 0) + jnp.where(has_outer, 2, 1)
    pl.semaphore_wait(barrier, waits)

    @pl.when(has_low)
    def _():
        for near in range(HALO):
            for k in range(own):
                density_low(k, near).start()

    @pl.when(has_high)
    def _():
        for near in range(HALO):
            for k in range(own):
                density_high(k, near).start()

    @pl.when(jnp.logical_not(has_low))
    def _():
        for buf in (dens, scal, quot):
            buf[:, 0:HALO] = jnp.zeros((own, HALO, nx, ny), jnp.float32)

    @pl.when(jnp.logical_not(has_high))
    def _():
        for buf in (dens, scal, quot):
            buf[:, nz + HALO :] = jnp.zeros((own, HALO, nx, ny), jnp.float32)

    for taps, size in ((band_x, nx), (band_y, ny)):
        whole = band(size)
        high = whole.astype(jnp.bfloat16)
        taps[0] = high
        taps[1] = (whole - high.astype(jnp.float32)).astype(jnp.bfloat16)
    at_x = lax.broadcasted_iota(jnp.int32, (nx, ny), 0)
    at_y = lax.broadcasted_iota(jnp.int32, (nx, ny), 1)
    inverse[...] = per_distance(jnp.minimum(at_x, nx - 1 - at_x)) * per_distance(
        jnp.minimum(at_y, ny - 1 - at_y)
    )

    count = weights.shape[0]
    weight_sum = weights[0]
    for k in range(1, count):
        weight_sum = weight_sum + weights[k]
    norm = [
        jnp.full((1, ny), weights[vol * own + k], jnp.float32)
        / jnp.full((1, ny), weight_sum, jnp.float32)
        for k in range(own)
    ]

    def split(value):
        high = value.astype(jnp.bfloat16)
        return high, (value - high.astype(jnp.float32)).astype(jnp.bfloat16)

    def dot(a, b):
        return jnp.dot(a, b, preferred_element_type=jnp.float32)

    def in_plane(value):
        high, low = split(value)
        blurred = dot(high, band_y[0]) + (dot(high, band_y[1]) + dot(low, band_y[0]))
        high, low = split(blurred)
        return dot(band_x[0], high) + (dot(band_x[1], high) + dot(band_x[0], low))

    def along_z(buf, k, p):
        total = kernel_taps[0] * (buf[k, p] + buf[k, p + 4])
        total = total + kernel_taps[1] * (buf[k, p + 1] + buf[k, p + 3])
        return total + kernel_taps[2] * buf[k, p + 2]

    def faces(i):
        near = 1 - i // 2
        return near + (i % 2) * (nz - 1 - 2 * near)

    def order_first(i):
        late, last = (i + nz - 2) // nz, (i + nz - 6) // nz
        return (1 - late) * (i + 2) + (late - last) * faces(jnp.maximum(i - 2, 0)) + last * (i - 2)

    def order_second(i):
        late = (i + 4) // nz
        return (1 - late) * (i + 2) + late * faces(jnp.maximum(i - (nz - 4), 0))

    def up_center(t, g):
        return remote(
            acc.at[t, g], inner.at[t, g], up_send.at[t, g], inner_recv.at[t, g], {"vol": inward}
        )

    def up_other(t, g):
        return remote(
            acc.at[t, g], outer.at[t, g], up_send.at[t, g], outer_recv.at[t, g], {"vol": inward}
        )

    def down_copy(t, g):
        return remote(
            inner.at[t, g], inner.at[t, g], down_send.at[t, g], inner_recv.at[t, g],
            {"vol": outward},
        )

    def up(t, g):
        @pl.when(has_outer)
        def _():
            up_other(t, g).wait_recv()
            acc[t, g] = acc[t, g] + outer[t, g]

        pl.when(is_center)(lambda: up_center(t, g).start())
        pl.when(jnp.logical_not(is_center))(lambda: up_other(t, g).start())

    def down(t, g, use):
        down_copy(t, g).wait_recv()

        @pl.when(is_center)
        def _():
            inner[t, g] = inner[t, g] + acc[t, g]

        pl.when(has_outer)(lambda: down_copy(t, g).start())
        use(g)

    def all_reduce(t, order, compute, use):
        def step(i, _):
            part = compute(i, order(i))
            for c in range(CHUNKS):
                acc[t, i * CHUNKS + c] = part[c * rows : (c + 1) * rows]

            def chunk(c, _):
                g = i * CHUNKS + c
                up(t, g)
                pl.when(g >= lag)(lambda: down(t, g - lag, use))
                return 0

            lax.fori_loop(0, CHUNKS, chunk, 0)
            return 0

        lax.fori_loop(0, nz, step, 0)

        def tail(g, _):
            down(t, g, use)
            return 0

        lax.fori_loop(steps - lag, steps, tail, 0)

    def weighted(k, value):
        return norm[k] * jnp.log(value)

    for load in loads:
        load.wait()

    def first_compute(i, p):
        for near in range(HALO):
            @pl.when(jnp.logical_and(i == 2 + 2 * near, has_low))
            def _():
                for k in range(own):
                    density_high(k, near).wait_recv()

            @pl.when(jnp.logical_and(i == 2 + 2 * near, has_high))
            def _():
                for k in range(own):
                    density_low(k, near).wait_recv()

        scale = []
        for offset in range(5):
            z = slab * nz + p + offset - HALO
            scale.append(kernel_taps[offset] * per_distance(jnp.minimum(z, total_nz - 1 - z)))
        part = None
        for k in range(own):
            value = scale[0] * dens[k, p]
            for offset in range(1, 5):
                value = value + scale[offset] * dens[k, p + offset]
            spread = in_plane(value * inverse[...])
            marg[k, p] = spread
            term = weighted(k, spread)
            part = term if part is None else part + term
        return part

    def send_face(buf, send, recv, p):
        @pl.when(jnp.logical_and(has_low, p < HALO))
        def _():
            for k in range(own):
                plane_low(buf, send, recv, k, p).start()

        @pl.when(jnp.logical_and(has_high, p >= nz - HALO))
        def _():
            for k in range(own):
                plane_high(buf, send, recv, k, p).start()

    def wait_low(buf, send, recv):
        @pl.when(has_low)
        def _():
            for k in range(own):
                for p in range(nz - HALO, nz):
                    plane_high(buf, send, recv, k, p).wait_recv()

    def wait_high(buf, send, recv):
        @pl.when(has_high)
        def _():
            for k in range(own):
                for p in range(HALO):
                    plane_low(buf, send, recv, k, p).wait_recv()

    def wait_sent(buf, send, recv):
        @pl.when(has_low)
        def _():
            for k in range(own):
                for p in range(HALO):
                    plane_low(buf, send, recv, k, p).wait_send()

        @pl.when(has_high)
        def _():
            for k in range(own):
                for p in range(nz - HALO, nz):
                    plane_high(buf, send, recv, k, p).wait_send()

    def quotient(p):
        for k in range(own):
            quot[k, p + HALO] = dens[k, p + HALO] / in_plane(along_z(scal, k, p))
        send_face(quot, q_send, q_recv, p)

    def quotients(start, stop):
        def one(p, _):
            quotient(p)
            return 0

        lax.fori_loop(start, stop, one, 0)

    def quotients_low():
        wait_low(scal, s_send, s_recv)
        quotients(0, HALO)

    def first_use(g):
        i, c = g // CHUNKS, g % CHUNKS
        p = order_first(i)
        at = pl.ds(pl.multiple_of(c * rows, rows), rows)
        center = jnp.exp(inner[0, g])
        for k in range(own):
            scal[k, p + HALO, at] = center / marg[k, p, at]

        @pl.when(c == CHUNKS - 1)
        def _():
            send_face(scal, s_send, s_recv, p)
            pl.when(jnp.logical_and(i == nz - 2, early))(quotients_low)

    all_reduce(0, order_first, first_compute, first_use)

    pl.when(jnp.logical_not(early))(quotients_low)
    quotients(HALO, HALO + 3)
    wait_high(scal, s_send, s_recv)
    quotients(nz - 1, nz)

    def second_compute(i, p):
        @pl.when(jnp.logical_and(i >= 1, i < nz - 5))
        def _():
            quotient(i + 4)

        @pl.when(i == nz - 4)
        def _():
            wait_low(quot, q_send, q_recv)
            wait_high(quot, q_send, q_recv)

        part = None
        for k in range(own):
            marginal = scal[k, p + HALO] * in_plane(along_z(quot, k, p))
            marg[k, p] = marginal
            term = weighted(k, marginal)
            part = term if part is None else part + term
        return part

    def center_store(p):
        return pltpu.make_async_copy(cent.at[p], center_out.at[p], out_sem.at[own, p])

    def scaling_store(k, p):
        return pltpu.make_async_copy(marg.at[k, p], scaling_out.at[k, p], out_sem.at[k, p])

    def second_use(g):
        p, c = order_second(g // CHUNKS), g % CHUNKS
        at = pl.ds(pl.multiple_of(c * rows, rows), rows)
        center = jnp.exp(inner[1, g])
        cent[p, at] = center
        for k in range(own):
            marg[k, p, at] = scal[k, p + HALO, at] * center / marg[k, p, at]

        @pl.when(c == CHUNKS - 1)
        def _():
            center_store(p).start()
            for k in range(own):
                scaling_store(k, p).start()

    all_reduce(1, order_second, second_compute, second_use)

    @pl.when(has_low)
    def _():
        for near in range(HALO):
            for k in range(own):
                density_low(k, near).wait_send()

    @pl.when(has_high)
    def _():
        for near in range(HALO):
            for k in range(own):
                density_high(k, near).wait_send()

    wait_sent(scal, s_send, s_recv)
    wait_sent(quot, q_send, q_recv)

    def drain(g, _):
        for t in range(ITERS):
            up_other(t, g).wait_send()
            pl.when(has_outer)(lambda: down_copy(t, g).wait_send())
        return 0

    lax.fori_loop(0, steps, drain, 0)

    def stored(p, _):
        center_store(p).wait()
        for k in range(own):
            scaling_store(k, p).wait()
        return 0

    lax.fori_loop(0, nz, stored, 0)


def per_device(slabs, vols, density, weights):
    own, nz, nx, ny = density.shape
    steps, rows = nz * CHUNKS, nx // CHUNKS
    padded = pltpu.VMEM((own, nz + 2 * HALO, nx, ny), jnp.float32)
    chunks = pltpu.VMEM((ITERS, steps, rows, ny), jnp.float32)
    dma = pltpu.SemaphoreType.DMA
    return pl.pallas_call(
        functools.partial(kernel, slabs, vols),
        out_shape=(
            jax.ShapeDtypeStruct((nz, nx, ny), jnp.float32),
            jax.ShapeDtypeStruct(density.shape, jnp.float32),
        ),
        in_specs=[pl.BlockSpec(memory_space=pltpu.SMEM), pl.BlockSpec(memory_space=pl.ANY)],
        out_specs=(pl.BlockSpec(memory_space=pl.ANY), pl.BlockSpec(memory_space=pl.ANY)),
        scratch_shapes=[
            padded, padded, padded,
            pltpu.VMEM((own, nz, nx, ny), jnp.float32),
            pltpu.VMEM((nz, nx, ny), jnp.float32),
            chunks, chunks, chunks,
            pltpu.VMEM((nx, ny), jnp.float32),
            pltpu.VMEM((2, nx, nx), jnp.bfloat16),
            pltpu.VMEM((2, ny, ny), jnp.bfloat16),
            dma((own,)), dma((own + 1, nz)),
            dma((2, own, HALO)), dma((2, own, HALO)),
            dma((2, own, HALO)), dma((2, own, HALO)),
            dma((2, own, HALO)), dma((2, own, HALO)),
            dma((ITERS, steps)), dma((ITERS, steps)),
            dma((ITERS, steps)), dma((ITERS, steps)),
        ],
        compiler_params=pltpu.CompilerParams(
            collective_id=0, has_side_effects=True, vmem_limit_bytes=52 * 1024 * 1024
        ),
    )(weights, density)


def solution(mesh):
    in_specs = (P(("groups", "vol"), "slab", None, None), P("groups"))
    out_specs = (P(("groups", "slab"), None, None), P(("groups", "vol"), "slab", None, None))
    body = functools.partial(per_device, mesh.shape["slab"], mesh.shape["vol"])
    return jax.shard_map(
        body, mesh=mesh, in_specs=in_specs, out_specs=out_specs, check_vma=False
    )
```

```python
import functools

import jax
import jax.numpy as jnp
import numpy as np
from jax import lax
from jax.experimental import pallas as pl
from jax.experimental.pallas import tpu as pltpu
from jax.sharding import PartitionSpec as P

ITERS = 2
HALO = 2
CHUNKS = 4

gauss_raw = np.exp(-0.5 * np.arange(-2, 3) ** 2)
kernel_taps = [float(entry) for entry in gauss_raw / gauss_raw.sum()]
edge_sums = [sum(kernel_taps[2:]), sum(kernel_taps[1:]), sum(kernel_taps)]


def per_distance(distance):
    inverse = [1.0 / entry for entry in edge_sums]
    inner = jnp.where(distance == 1, inverse[1], inverse[2])
    return jnp.where(distance == 0, inverse[0], inner).astype(jnp.float32)


def band(size):
    rows = lax.broadcasted_iota(jnp.int32, (size, size), 0)
    gap = jnp.abs(rows - lax.broadcasted_iota(jnp.int32, (size, size), 1))
    inner = jnp.where(gap == 1, kernel_taps[1], jnp.where(gap == 2, kernel_taps[0], 0.0))
    return jnp.where(gap == 0, kernel_taps[2], inner).astype(jnp.float32)


def kernel(
    slabs, vols,
    weights, density, center_out, scaling_out,
    dens, scal, quot, marg, cent, acc, outer, inner, inverse, band_x, band_y,
    local_sem, out_sem, d_send, d_recv, s_send, s_recv, q_send, q_recv,
    up_send, down_send, outer_recv, inner_recv,
):
    own, nz, nx, ny = density.shape
    total_nz = nz * slabs
    rows = nx // CHUNKS
    steps = nz * CHUNKS
    slab, vol = lax.axis_index("slab"), lax.axis_index("vol")
    half = vols // 2
    low_side = vol < half
    inward = jnp.where(low_side, vol + 1, vol - 1)
    outward = jnp.where(low_side, vol - 1, vol + 1)
    depth = jnp.where(low_side, half - 1 - vol, vol - half)
    is_center = depth == 0
    early = depth > 0
    has_outer = depth < half - 1
    lag = jnp.minimum(3 + 9 * depth, steps)
    has_low, has_high = slab > 0, slab < slabs - 1

    barrier = pltpu.get_barrier_semaphore()

    def greet(device):
        pl.semaphore_signal(barrier, inc=1, device_id=device, device_id_type=pl.DeviceIdType.MESH)

    pl.when(has_low)(lambda: greet({"slab": slab - 1}))
    pl.when(has_high)(lambda: greet({"slab": slab + 1}))
    greet({"vol": inward})
    pl.when(has_outer)(lambda: greet({"vol": outward}))

    loads = [
        pltpu.make_async_copy(density.at[k], dens.at[k, pl.ds(HALO, nz)], local_sem.at[k])
        for k in range(own)
    ]
    for load in loads:
        load.start()

    def remote(src, dst, send, recv, device):
        return pltpu.make_async_remote_copy(
            src_ref=src, dst_ref=dst, send_sem=send, recv_sem=recv,
            device_id=device, device_id_type=pl.DeviceIdType.MESH,
        )

    def density_low(k, near):
        return remote(
            density.at[k, near], dens.at[k, nz + HALO + near],
            d_send.at[0, k, near], d_recv.at[0, k, near], {"slab": slab - 1},
        )

    def density_high(k, near):
        return remote(
            density.at[k, nz - 1 - near], dens.at[k, HALO - 1 - near],
            d_send.at[1, k, near], d_recv.at[1, k, near], {"slab": slab + 1},
        )

    def plane_low(buf, send, recv, k, p):
        return remote(
            buf.at[k, p + HALO], buf.at[k, p + HALO + nz],
            send.at[0, k, p], recv.at[0, k, p], {"slab": slab - 1},
        )

    def plane_high(buf, send, recv, k, p):
        at = p - (nz - HALO)
        return remote(
            buf.at[k, p + HALO], buf.at[k, at],
            send.at[1, k, at], recv.at[1, k, at], {"slab": slab + 1},
        )

    waits = jnp.where(has_low, 1, 0) + jnp.where(has_high, 1, 0) + jnp.where(has_outer, 2, 1)
    pl.semaphore_wait(barrier, waits)

    @pl.when(has_low)
    def _():
        for near in range(HALO):
            for k in range(own):
                density_low(k, near).start()

    @pl.when(has_high)
    def _():
        for near in range(HALO):
            for k in range(own):
                density_high(k, near).start()

    @pl.when(jnp.logical_not(has_low))
    def _():
        for buf in (dens, scal, quot):
            buf[:, 0:HALO] = jnp.zeros((own, HALO, nx, ny), jnp.float32)

    @pl.when(jnp.logical_not(has_high))
    def _():
        for buf in (dens, scal, quot):
            buf[:, nz + HALO :] = jnp.zeros((own, HALO, nx, ny), jnp.float32)

    for taps, size in ((band_x, nx), (band_y, ny)):
        whole = band(size)
        high = whole.astype(jnp.bfloat16)
        taps[0] = high
        taps[1] = (whole - high.astype(jnp.float32)).astype(jnp.bfloat16)
    at_x = lax.broadcasted_iota(jnp.int32, (nx, ny), 0)
    at_y = lax.broadcasted_iota(jnp.int32, (nx, ny), 1)
    inverse[...] = per_distance(jnp.minimum(at_x, nx - 1 - at_x)) * per_distance(
        jnp.minimum(at_y, ny - 1 - at_y)
    )

    count = weights.shape[0]
    weight_sum = weights[0]
    for k in range(1, count):
        weight_sum = weight_sum + weights[k]
    norm = [
        jnp.full((1, ny), weights[vol * own + k], jnp.float32)
        / jnp.full((1, ny), weight_sum, jnp.float32)
        for k in range(own)
    ]

    def split(value):
        high = value.astype(jnp.bfloat16)
        return high, (value - high.astype(jnp.float32)).astype(jnp.bfloat16)

    def dot(a, b):
        return jnp.dot(a, b, preferred_element_type=jnp.float32)

    def in_plane(value):
        high, low = split(value)
        blurred = dot(high, band_y[0]) + (dot(high, band_y[1]) + dot(low, band_y[0]))
        high, low = split(blurred)
        return dot(band_x[0], high) + (dot(band_x[1], high) + dot(band_x[0], low))

    def along_z(buf, k, p):
        total = kernel_taps[0] * (buf[k, p] + buf[k, p + 4])
        total = total + kernel_taps[1] * (buf[k, p + 1] + buf[k, p + 3])
        return total + kernel_taps[2] * buf[k, p + 2]

    def faces(i):
        near = 1 - i // 2
        return near + (i % 2) * (nz - 1 - 2 * near)

    def order_first(i):
        late, last = (i + nz - 2) // nz, (i + nz - 6) // nz
        return (1 - late) * (i + 2) + (late - last) * faces(jnp.maximum(i - 2, 0)) + last * (i - 2)

    def order_second(i):
        late = (i + 4) // nz
        return (1 - late) * (i + 2) + late * faces(jnp.maximum(i - (nz - 4), 0))

    def up_center(t, g):
        return remote(
            acc.at[t, g], inner.at[t, g], up_send.at[t, g], inner_recv.at[t, g], {"vol": inward}
        )

    def up_other(t, g):
        return remote(
            acc.at[t, g], outer.at[t, g], up_send.at[t, g], outer_recv.at[t, g], {"vol": inward}
        )

    def down_copy(t, g):
        return remote(
            inner.at[t, g], inner.at[t, g], down_send.at[t, g], inner_recv.at[t, g],
            {"vol": outward},
        )

    def up(t, g):
        @pl.when(has_outer)
        def _():
            up_other(t, g).wait_recv()
            acc[t, g] = acc[t, g] + outer[t, g]

        pl.when(is_center)(lambda: up_center(t, g).start())
        pl.when(jnp.logical_not(is_center))(lambda: up_other(t, g).start())

    def down(t, g, use):
        down_copy(t, g).wait_recv()

        @pl.when(is_center)
        def _():
            inner[t, g] = inner[t, g] + acc[t, g]

        pl.when(has_outer)(lambda: down_copy(t, g).start())
        use(g)

    def all_reduce(t, order, compute, use):
        def step(i, _):
            part = compute(i, order(i))
            for c in range(CHUNKS):
                acc[t, i * CHUNKS + c] = part[c * rows : (c + 1) * rows]

            def chunk(c, _):
                g = i * CHUNKS + c
                up(t, g)
                pl.when(g >= lag)(lambda: down(t, g - lag, use))
                return 0

            lax.fori_loop(0, CHUNKS, chunk, 0)
            return 0

        lax.fori_loop(0, nz, step, 0)

        def tail(g, _):
            down(t, g, use)
            return 0

        lax.fori_loop(steps - lag, steps, tail, 0)

    def weighted(k, value):
        return norm[k] * jnp.log(value)

    for load in loads:
        load.wait()

    def first_compute(i, p):
        for near in range(HALO):
            @pl.when(jnp.logical_and(i == 2 + 2 * near, has_low))
            def _():
                for k in range(own):
                    density_high(k, near).wait_recv()

            @pl.when(jnp.logical_and(i == 2 + 2 * near, has_high))
            def _():
                for k in range(own):
                    density_low(k, near).wait_recv()

        scale = []
        for offset in range(5):
            z = slab * nz + p + offset - HALO
            scale.append(kernel_taps[offset] * per_distance(jnp.minimum(z, total_nz - 1 - z)))
        part = None
        for k in range(own):
            value = scale[0] * dens[k, p]
            for offset in range(1, 5):
                value = value + scale[offset] * dens[k, p + offset]
            spread = in_plane(value * inverse[...])
            marg[k, p] = spread
            term = weighted(k, spread)
            part = term if part is None else part + term
        return part

    def send_face(buf, send, recv, p):
        @pl.when(jnp.logical_and(has_low, p < HALO))
        def _():
            for k in range(own):
                plane_low(buf, send, recv, k, p).start()

        @pl.when(jnp.logical_and(has_high, p >= nz - HALO))
        def _():
            for k in range(own):
                plane_high(buf, send, recv, k, p).start()

    def wait_low(buf, send, recv):
        @pl.when(has_low)
        def _():
            for k in range(own):
                for p in range(nz - HALO, nz):
                    plane_high(buf, send, recv, k, p).wait_recv()

    def wait_high(buf, send, recv):
        @pl.when(has_high)
        def _():
            for k in range(own):
                for p in range(HALO):
                    plane_low(buf, send, recv, k, p).wait_recv()

    def wait_sent(buf, send, recv):
        @pl.when(has_low)
        def _():
            for k in range(own):
                for p in range(HALO):
                    plane_low(buf, send, recv, k, p).wait_send()

        @pl.when(has_high)
        def _():
            for k in range(own):
                for p in range(nz - HALO, nz):
                    plane_high(buf, send, recv, k, p).wait_send()

    def quotient(p):
        for k in range(own):
            quot[k, p + HALO] = dens[k, p + HALO] / in_plane(along_z(scal, k, p))
        send_face(quot, q_send, q_recv, p)

    def quotients(start, stop):
        def one(p, _):
            quotient(p)
            return 0

        lax.fori_loop(start, stop, one, 0)

    def quotients_low():
        wait_low(scal, s_send, s_recv)
        quotients(0, HALO)

    def first_use(g):
        i, c = g // CHUNKS, g % CHUNKS
        p = order_first(i)
        at = pl.ds(pl.multiple_of(c * rows, rows), rows)
        center = jnp.exp(inner[0, g])
        for k in range(own):
            scal[k, p + HALO, at] = center / marg[k, p, at]

        @pl.when(c == CHUNKS - 1)
        def _():
            send_face(scal, s_send, s_recv, p)
            pl.when(jnp.logical_and(i == nz - 2, early))(quotients_low)

    all_reduce(0, order_first, first_compute, first_use)

    pl.when(jnp.logical_not(early))(quotients_low)
    quotients(HALO, HALO + 3)
    wait_high(scal, s_send, s_recv)
    quotients(nz - 1, nz)

    def second_compute(i, p):
        @pl.when(jnp.logical_and(i >= 1, i < nz - 5))
        def _():
            quotient(i + 4)

        @pl.when(i == nz - 4)
        def _():
            wait_low(quot, q_send, q_recv)
            wait_high(quot, q_send, q_recv)

        part = None
        for k in range(own):
            marginal = scal[k, p + HALO] * in_plane(along_z(quot, k, p))
            marg[k, p] = marginal
            term = weighted(k, marginal)
            part = term if part is None else part + term
        return part

    def center_store(p):
        return pltpu.make_async_copy(cent.at[p], center_out.at[p], out_sem.at[own, p])

    def scaling_store(k, p):
        return pltpu.make_async_copy(marg.at[k, p], scaling_out.at[k, p], out_sem.at[k, p])

    def second_use(g):
        p, c = order_second(g // CHUNKS), g % CHUNKS
        at = pl.ds(pl.multiple_of(c * rows, rows), rows)
        center = jnp.exp(inner[1, g])
        cent[p, at] = center
        for k in range(own):
            marg[k, p, at] = scal[k, p + HALO, at] * center / marg[k, p, at]

        @pl.when(c == CHUNKS - 1)
        def _():
            center_store(p).start()
            for k in range(own):
                scaling_store(k, p).start()

    all_reduce(1, order_second, second_compute, second_use)

    @pl.when(has_low)
    def _():
        for near in range(HALO):
            for k in range(own):
                density_low(k, near).wait_send()

    @pl.when(has_high)
    def _():
        for near in range(HALO):
            for k in range(own):
                density_high(k, near).wait_send()

    wait_sent(scal, s_send, s_recv)
    wait_sent(quot, q_send, q_recv)

    def drain(g, _):
        for t in range(ITERS):
            up_other(t, g).wait_send()
            pl.when(has_outer)(lambda: down_copy(t, g).wait_send())
        return 0

    lax.fori_loop(0, steps, drain, 0)

    def stored(p, _):
        center_store(p).wait()
        for k in range(own):
            scaling_store(k, p).wait()
        return 0

    lax.fori_loop(0, nz, stored, 0)


def per_device(slabs, vols, density, weights):
    own, nz, nx, ny = density.shape
    steps, rows = nz * CHUNKS, nx // CHUNKS
    padded = pltpu.VMEM((own, nz + 2 * HALO, nx, ny), jnp.float32)
    chunks = pltpu.VMEM((ITERS, steps, rows, ny), jnp.float32)
    dma = pltpu.SemaphoreType.DMA
    return pl.pallas_call(
        functools.partial(kernel, slabs, vols),
        out_shape=(
            jax.ShapeDtypeStruct((nz, nx, ny), jnp.float32),
            jax.ShapeDtypeStruct(density.shape, jnp.float32),
        ),
        in_specs=[pl.BlockSpec(memory_space=pltpu.SMEM), pl.BlockSpec(memory_space=pl.ANY)],
        out_specs=(pl.BlockSpec(memory_space=pl.ANY), pl.BlockSpec(memory_space=pl.ANY)),
        scratch_shapes=[
            padded, padded, padded,
            pltpu.VMEM((own, nz, nx, ny), jnp.float32),
            pltpu.VMEM((nz, nx, ny), jnp.float32),
            chunks, chunks, chunks,
            pltpu.VMEM((nx, ny), jnp.float32),
            pltpu.VMEM((2, nx, nx), jnp.bfloat16),
            pltpu.VMEM((2, ny, ny), jnp.bfloat16),
            dma((own,)), dma((own + 1, nz)),
            dma((2, own, HALO)), dma((2, own, HALO)),
            dma((2, own, HALO)), dma((2, own, HALO)),
            dma((2, own, HALO)), dma((2, own, HALO)),
            dma((ITERS, steps)), dma((ITERS, steps)),
            dma((ITERS, steps)), dma((ITERS, steps)),
        ],
        compiler_params=pltpu.CompilerParams(
            collective_id=0, has_side_effects=True, vmem_limit_bytes=52 * 1024 * 1024
        ),
    )(weights, density)


def solution(mesh):
    in_specs = (P(("groups", "vol"), "slab", None, None), P("groups"))
    out_specs = (P(("groups", "slab"), None, None), P(("groups", "vol"), "slab", None, None))
    body = functools.partial(per_device, mesh.shape["slab"], mesh.shape["vol"])
    return jax.shard_map(
        body, mesh=mesh, in_specs=in_specs, out_specs=out_specs, check_vma=False
    )
```
